32 devices in a mesh: parts: 2 (over x), order: 8 (over z, y), lat: 2 (over core).
Axes of the slice: x: 2, y: 2, z: 4, core: 2. Of those that a mesh axis runs over, the one named last changes fastest.
Arguments:
- fourier: float32 [128, 16, 64, 128], P('parts', 'lat', 'order'), parts along dimension 0, may hold values from -6 to 6
- factors: float32 [64, 4, 16, 64, 128], P('order', None, 'lat'), may hold values from -0.5 to 0.5
- slot_of_order: int32 [64], replicated, may hold values from 0 to 63, each once
- ranks: int32 [64, 4], replicated, may hold values from 16 to 64
- pattern: int32 [64, 4, 16], replicated, may hold values 0 or 1
Outputs:
- spectra: float32 [128, 16, 64, 128], P(('parts', 'order'), 'lat'), parts along dimension 0
The draws below stay inside these ranges and needn't reach their ends.
There are 2 independent parts, one for each index of `parts`. The reference program is written for one: setup_inputs(seed, part) draws one part's arguments, and reference() takes and returns one part's arrays. A program takes and returns all parts, laid end to end along the dimension named above; an argument that names none is the same for every part. Nothing has to cross between parts.
All inputs are finite; a program needn't handle non-finite values.
Results may differ from the reference program's by a relative error of at most 0.0003.
Values sent between devices are 32-bit elements; how exact they have to be, the bound alone decides.
No kernel may reach another device: no remote copies, remote signals or barrier semaphores. Data moves between devices by JAX's collectives and lax.ppermute only.
A program may use at most 64 MiB of HBM per device.

```python
import jax
import jax.numpy as jnp
from jax import lax

COLS = 128
NB = 16
LEVELS = 4
LB = 64
SLOTS = 64
ORDERS = 64


def place_ends(array, key, low, top_value):
    longest = array.shape.index(max(array.shape))
    spots = []
    for shift in (0, 1):
        where = [jax.random.randint(jax.random.fold_in(key, axis), (), 0, length) for axis, length in enumerate(array.shape)]
        where[longest] = (where[longest] + shift) % array.shape[longest]
        spots.append(tuple(where))
    return array.at[spots[0]].set(low).at[spots[1]].set(top_value)


def level_of(stream_key, extent, cuts, smallest, high):
    factor_of, own = 1.0, jax.random.fold_in(stream_key, 6)
    for dim, parts in cuts:
        heights = jnp.exp(jax.random.uniform(jax.random.fold_in(own, dim), (parts,), jnp.float32, smallest / len(cuts), high / len(cuts)))
        factor_of = factor_of * jnp.repeat(heights, extent[dim] // parts).reshape([-1 if axis == dim else 1 for axis in range(len(extent))])
    return factor_of


def gaussian(key, extent, deviation, reach, cuts=(), kind=jnp.bfloat16):
    factor_of = level_of(key, extent, cuts, -0.22, 0.18) if cuts else 1.0
    entries = jax.random.normal(key, extent, jnp.float32) * deviation * factor_of
    return jnp.minimum(jnp.maximum(entries, -reach), reach).astype(kind)


def setup_inputs(seed: int = 0, part: int = 0) -> dict:
    key_of = jax.random.split(jax.random.key(seed), 6)
    own_keys = jax.random.split(jax.random.fold_in(key_of[5], part), 6)
    fourier = gaussian(own_keys[0], (ORDERS, NB, LB, COLS), 1.0, 6.0, ((1, 2), (2, 8)), jnp.float32)
    factors = gaussian(key_of[1], (SLOTS, LEVELS, NB, LB, 2 * LB), (2 * LB) ** -0.5, 0.5, ((0, 8), (2, 2)), jnp.float32)
    slot_of_order = jax.random.permutation(key_of[2], ORDERS).astype(jnp.int32)
    ranks = place_ends(jax.random.randint(key_of[3], (ORDERS, LEVELS), LB // 4, LB + 1), jax.random.fold_in(key_of[3], 1), LB // 4, LB).astype(jnp.int32)
    pattern = place_ends((jax.random.randint(key_of[4], (ORDERS, LEVELS, NB), 0, 4) < 3).astype(jnp.int32), jax.random.fold_in(key_of[4], 1), 0, 1)
    return dict(fourier=fourier, factors=factors, slot_of_order=slot_of_order, ranks=ranks, pattern=pattern)


def reference(fourier, factors, slot_of_order, ranks, pattern):
    every_slot = jnp.arange(SLOTS, dtype=jnp.int32)
    hit_table = (slot_of_order[None, :] == every_slot[:, None]).astype(jnp.int32)
    lanes = jnp.arange(LB, dtype=jnp.int32)

    def one_slot(slot):
        hits = hit_table[slot]
        state = jnp.tensordot(hits.astype(jnp.float32), fourier, axes=1, precision=lax.Precision.HIGHEST)
        slot_rank = jnp.sum(hits[:, None] * ranks, axis=0)
        slot_pattern = jnp.sum(hits[:, None, None] * pattern, axis=0)
        for level in range(LEVELS):
            dist = NB >> (level + 1)
            shaped = state.reshape(NB // (2 * dist), 2, dist, LB, COLS)
            partner = jnp.flip(shaped, axis=1).reshape(NB, LB, COLS)
            keep = (lanes < slot_rank[level]).astype(jnp.float32)
            pair_mask = keep[None, :] * slot_pattern[level][:, None].astype(jnp.float32)
            mask = jnp.concatenate([jnp.ones((NB, LB), jnp.float32), pair_mask], axis=1)
            matrix = factors[slot, level] * mask[:, None, :]
            stacked = jnp.concatenate([state, partner], axis=1)
            state = jnp.einsum("bpq,bqn->bpn", matrix, stacked, precision=lax.Precision.HIGHEST)
        return state

    return lax.map(one_slot, every_slot)
```

```python
import functools

import jax
import jax.numpy as jnp
from jax import lax
from jax.experimental import pallas as pl
from jax.experimental.pallas import tpu as pltpu
from jax.sharding import PartitionSpec as P

LEVELS = 4
CHUNKS = (6, 2)
ANY = pl.BlockSpec(memory_space=pl.ANY)
SMEM = pl.BlockSpec(memory_space=pltpu.SMEM)
VMEM = pl.BlockSpec(memory_space=pltpu.VMEM)


def in_vmem(x):
    return pltpu.with_memory_space_constraint(x, pltpu.VMEM)


def in_hbm(x):
    return pltpu.with_memory_space_constraint(x, pltpu.HBM)


def gather_kernel(plan, slot_count, n_after, slot_ref, rows_ref, *refs):
    refs = refs[n_after:]
    outs, (inverse, sems) = refs[: len(plan)], refs[len(plan) :]
    me = lax.axis_index("order")

    def invert(m, carry):
        inverse[slot_ref[m]] = m
        return carry

    lax.fori_loop(0, slot_ref.shape[0], invert, 0)
    for o, (hop, first, count) in enumerate(plan):
        base = (me ^ hop) * slot_count + first

        def issue(t, carry, o=o, base=base):
            pltpu.make_async_copy(
                rows_ref.at[inverse[base + t]], outs[o].at[t], sems.at[o]
            ).start()
            return carry

        lax.fori_loop(0, count, issue, 0, unroll=True)
    for o in range(len(plan)):
        pltpu.make_async_copy(outs[o], outs[o], sems.at[o]).wait()


def gather(plan, slot_count, slot_of_order, fourier, after=()):
    shapes = [pltpu.VMEM((count,) + fourier.shape[1:], fourier.dtype) for _, _, count in plan]
    size = sum(count for _, _, count in plan) * fourier[0].size * 4
    return pl.pallas_call(
        functools.partial(gather_kernel, plan, slot_count, len(after)),
        out_shape=shapes,
        in_specs=[SMEM, ANY] + [ANY] * len(after),
        out_specs=[VMEM] * len(plan),
        scratch_shapes=[
            pltpu.SMEM((slot_of_order.shape[0],), jnp.int32),
            pltpu.SemaphoreType.DMA((len(plan),)),
        ],
        compiler_params=pltpu.CompilerParams(vmem_limit_bytes=4 * 1024 * 1024),
        cost_estimate=pl.CostEstimate(flops=0, bytes_accessed=2 * size, transcendentals=0),
        name="gather_rows",
    )(slot_of_order, in_hbm(fourier), *after)


def join_kernel(plan, count, *refs):
    pieces, out = refs[: len(plan)], refs[len(plan)]
    me = lax.axis_index("order")
    for piece, (hop, first) in zip(pieces, plan):
        rows = piece.shape[2]
        low = pl.multiple_of((me ^ hop) * rows, rows)
        out[:, :, pl.ds(low, rows), :] = piece[first : first + count]


def join(plan, count, pieces):
    _, blocks, rows, columns = pieces[0].shape
    shape = (count, blocks, rows * len(plan), columns)
    size = 4 * count * blocks * rows * len(plan) * columns
    return pl.pallas_call(
        functools.partial(join_kernel, plan, count),
        out_shape=pltpu.VMEM(shape, pieces[0].dtype),
        in_specs=[VMEM] * len(plan),
        out_specs=VMEM,
        compiler_params=pltpu.CompilerParams(vmem_limit_bytes=4 * 1024 * 1024),
        cost_estimate=pl.CostEstimate(flops=0, bytes_accessed=2 * size, transcendentals=0),
        name="join_rows",
    )(*[in_vmem(piece) for piece in pieces])


def halves(x):
    high = x.astype(jnp.bfloat16)
    return high, (x - high.astype(jnp.float32)).astype(jnp.bfloat16)


def product(matrix, stacked):
    n = stacked.shape[1]
    high, low = halves(stacked)
    wide = jnp.concatenate([high, low], axis=1)
    wide = jnp.concatenate([wide, wide], axis=0)
    out = jnp.dot(
        jnp.concatenate(halves(matrix), axis=1), wide, preferred_element_type=jnp.float32
    )
    return out[:, :n] + out[:, n:]


def butterfly_kernel(first, bound_ref, factor_ref, own_ref, partner_ref, *refs):
    out_ref = refs[-1]
    _, levels, blocks, rows, width = factor_ref.shape
    here = pl.program_id(0)
    slot = here + first
    lanes = lax.broadcasted_iota(jnp.int32, (rows, width), 1)

    def matrix(level, i):
        keep = lanes < bound_ref[(slot * levels + level) * blocks + i]
        return jnp.where(keep, factor_ref[0, level, i], 0.0)

    state = []
    for i in range(blocks):
        stacked = jnp.concatenate([own_ref[here, i], partner_ref[here, i]], axis=0)
        state.append(product(matrix(0, i), stacked))
    for level in range(1, levels):
        dist = blocks >> level
        new = [None] * blocks
        for i in range(blocks):
            j = i ^ dist
            if j < i:
                continue
            stacked = jnp.concatenate([state[i], state[j]], axis=0)
            other = pltpu.roll(matrix(level, j), rows, 1)
            both = product(jnp.concatenate([matrix(level, i), other], axis=0), stacked)
            new[i], new[j] = both[:rows], both[rows:]
        state = new
    for i in range(blocks):
        out_ref[0, i] = state[i]


def butterfly(first, bound, factors, own, partner, so_far):
    count, blocks, rows, columns = own.shape
    slot_count, levels = factors.shape[:2]
    width = factors.shape[4]
    in_specs = [
        SMEM,
        pl.BlockSpec((1, levels, blocks, rows, width), lambda s: (s + first, 0, 0, 0, 0)),
        VMEM,
        VMEM,
    ]
    args = [bound, in_hbm(factors), in_vmem(own), in_vmem(partner)]
    if so_far is not None:
        in_specs.append(ANY)
        args.append(so_far)
    return pl.pallas_call(
        functools.partial(butterfly_kernel, first),
        grid=(count,),
        out_shape=jax.ShapeDtypeStruct((slot_count, blocks, rows, columns), own.dtype),
        in_specs=in_specs,
        out_specs=pl.BlockSpec((1, blocks, rows, columns), lambda s: (s + first, 0, 0, 0)),
        input_output_aliases={} if so_far is None else {4: 0},
        compiler_params=pltpu.CompilerParams(vmem_limit_bytes=16 * 1024 * 1024),
        cost_estimate=pl.CostEstimate(
            flops=count * levels * blocks * rows * width * columns * 8,
            bytes_accessed=4 * count * blocks * rows * (levels * width + 3 * columns),
            transcendentals=0,
        ),
        name="butterfly",
    )(*args)


def coupling_bounds(slot_of_order, ranks, pattern, slot_count, blocks, rows):
    my_slots = lax.axis_index("order") * slot_count + jnp.arange(slot_count, dtype=jnp.int32)
    hits = (slot_of_order[None, :] == my_slots[:, None]).astype(jnp.int32)
    slot_rank = jnp.sum(hits[:, :, None] * ranks[None], axis=1)
    mine = lax.dynamic_slice_in_dim(pattern, lax.axis_index("lat") * blocks, blocks, 2)
    slot_pattern = jnp.sum(hits[:, :, None, None] * mine[None], axis=1)
    return (rows + slot_pattern * slot_rank[:, :, None]).reshape(-1)


def per_device(fourier, factors, slot_of_order, ranks, pattern):
    slot_count, _, blocks, block_rows, _ = factors.shape
    rows = fourier.shape[2]
    groups = lax.axis_size("order")
    bound = coupling_bounds(slot_of_order, ranks, pattern, slot_count, blocks, block_rows)
    swap = [(0, 1), (1, 0)]

    if rows % 8 or groups > 8 or groups & (groups - 1) or sum(CHUNKS) != slot_count:
        (packed,) = gather(((0, 0, slot_of_order.shape[0]),), 0, slot_of_order, fourier)
        own = lax.all_to_all(packed, "order", split_axis=0, concat_axis=2, tiled=True)
        return butterfly(0, bound, factors, own, lax.ppermute(own, "lat", swap), None)

    def hop(piece, k):
        return lax.ppermute(piece, "order", [(g, g ^ k) for g in range(groups)])

    near = list(range(1, groups // 2))
    far = list(range(groups // 2, groups))
    firsts = [sum(CHUNKS[:c]) for c in range(len(CHUNKS))]
    sent = gather([(k, 0, CHUNKS[0]) for k in far], slot_count, slot_of_order, fourier)
    far_pieces = [[hop(piece, k) for piece, k in zip(sent, far)]]
    plan = [(k, 0, slot_count) for k in [0] + near]
    for first, count in zip(firsts[1:], CHUNKS[1:]):
        plan += [(k, first, count) for k in far]
    sent = gather(plan, slot_count, slot_of_order, fourier)
    near_pieces = [sent[0]] + [hop(piece, k) for piece, k in zip(sent[1:], near)]
    rest = sent[len(near_pieces) :]
    for c in range(1, len(CHUNKS)):
        far_pieces.append([hop(piece, k) for piece, k in zip(rest, far)])
        rest = rest[len(far) :]
    out = None
    for first, count, pieces in zip(firsts, CHUNKS, far_pieces):
        plan = [(k, first) for k in [0] + near] + [(k, 0) for k in far]
        own = join(plan, count, near_pieces + pieces)
        out = butterfly(first, bound, factors, own, lax.ppermute(own, "lat", swap), out)
    return out


def solution(mesh):
    return jax.shard_map(
        per_device,
        mesh=mesh,
        in_specs=(
            P("parts", "lat", "order", None),
            P("order", None, "lat", None, None),
            P(),
            P(),
            P(),
        ),
        out_specs=P(("parts", "order"), "lat", None, None),
        check_vma=False,
    )
```

```python
import functools

import jax
import jax.numpy as jnp
from jax import lax
from jax.experimental import pallas as pl
from jax.experimental.pallas import tpu as pltpu
from jax.sharding import PartitionSpec as P

LEVELS = 4
CHUNKS = ((0, 6), (6, 2))
FAR = ((0, 0, 6, 0, None), (1, 0, 6, 0, None), (2, 0, 6, 0, 0), (3, 0, 6, 0, 1), (0, 6, 2, 1, 2), (1, 6, 2, 1, 3), (2, 6, 2, 1, -1), (3, 6, 2, 1, -1))
TOGETHER = 3
EARLY = None
US = 10**9
COUPLE_FLOPS = 30 * US
BUTTERFLY_FLOPS = 0
JOIN_FLOPS = 30 * US
ANY = pl.BlockSpec(memory_space=pl.ANY)
SMEM = pl.BlockSpec(memory_space=pltpu.SMEM)
VMEM = pl.BlockSpec(memory_space=pltpu.VMEM)


def in_vmem(x):
    return pltpu.with_memory_space_constraint(x, pltpu.VMEM)


def in_hbm(x):
    return pltpu.with_memory_space_constraint(x, pltpu.HBM)


def gather_kernel(plan, slot_count, n_after, slot_ref, rows_ref, *refs):
    refs = refs[n_after:]
    outs, (slots, inverse, load_sem, sems) = refs[: len(plan)], refs[len(plan) :]
    me = lax.axis_index("order")
    load = pltpu.make_async_copy(slot_ref, slots, load_sem)
    load.start()
    load.wait()

    def invert(m, carry):
        inverse[slots[m]] = m
        return carry

    lax.fori_loop(0, slots.shape[0], invert, 0, unroll=16)
    for o, (hop, first, count) in enumerate(plan):
        base = (me ^ hop) * slot_count + first

        def issue(t, carry, o=o, base=base):
            pltpu.make_async_copy(
                rows_ref.at[inverse[base + t]], outs[o].at[t], sems.at[o]
            ).start()
            return carry

        lax.fori_loop(0, count, issue, 0, unroll=True)
    for o in range(len(plan)):
        pltpu.make_async_copy(outs[o], outs[o], sems.at[o]).wait()


def gather(plan, slot_count, slot_of_order, fourier, after=()):
    shapes = [pltpu.VMEM((count,) + fourier.shape[1:], fourier.dtype) for _, _, count in plan]
    size = sum(count for _, _, count in plan) * fourier[0].size * 4
    return pl.pallas_call(
        functools.partial(gather_kernel, plan, slot_count, len(after)),
        out_shape=shapes,
        in_specs=[ANY, ANY] + [ANY] * len(after),
        out_specs=[VMEM] * len(plan),
        scratch_shapes=[
            pltpu.SMEM(slot_of_order.shape, jnp.int32),
            pltpu.SMEM(slot_of_order.shape, jnp.int32),
            pltpu.SemaphoreType.DMA,
            pltpu.SemaphoreType.DMA((len(plan),)),
        ],
        compiler_params=pltpu.CompilerParams(vmem_limit_bytes=4 * 1024 * 1024),
        cost_estimate=pl.CostEstimate(flops=0, bytes_accessed=2 * size, transcendentals=0),
        name="gather_rows",
    )(in_hbm(slot_of_order), in_hbm(fourier), *after)


def join_kernel(plan, count, *refs):
    pieces, out = refs[: len(plan)], refs[-1]
    me = lax.axis_index("order")
    for piece, (hop, first) in zip(pieces, plan):
        rows = piece.shape[2]
        low = pl.multiple_of((me ^ hop) * rows, rows)
        out[:, :, pl.ds(low, rows), :] = piece[first : first + count]


def join(plan, count, pieces, before, heavy):
    _, blocks, rows, columns = pieces[0].shape
    shape = (count, blocks, rows * len(plan), columns)
    size = 4 * count * blocks * rows * len(plan) * columns
    return pl.pallas_call(
        functools.partial(join_kernel, plan, count),
        out_shape=pltpu.VMEM(shape, pieces[0].dtype),
        in_specs=[VMEM] * len(plan) + [ANY] * len(before),
        out_specs=VMEM,
        compiler_params=pltpu.CompilerParams(vmem_limit_bytes=4 * 1024 * 1024),
        cost_estimate=pl.CostEstimate(
            flops=JOIN_FLOPS * heavy, bytes_accessed=2 * size, transcendentals=0
        ),
        name="join_rows",
    )(*[in_vmem(piece) for piece in pieces], *before)


def after(x, done):
    return lax.optimization_barrier((x, done))[0]


def halves(x):
    high = x.astype(jnp.bfloat16)
    return high, (x - high.astype(jnp.float32)).astype(jnp.bfloat16)


def couple_kernel(bound_ref, factor_ref, out_ref):
    slot = pl.program_id(0)
    _, levels, blocks, rows, width = factor_ref.shape
    lanes = lax.broadcasted_iota(jnp.int32, (rows, width), 1)
    for level in range(levels):
        for i in range(blocks):
            keep = lanes < bound_ref[(slot * levels + level) * blocks + i]
            matrix = jnp.where(keep, factor_ref[0, level, i], 0.0)
            if level and i & (blocks >> level):
                matrix = pltpu.roll(matrix, rows, 1)
            high, low = halves(matrix)
            out_ref[slot, level, i, :, :width] = high
            out_ref[slot, level, i, :, width:] = low


def couple(bound, factors):
    slot_count, levels, blocks, rows, width = factors.shape
    return pl.pallas_call(
        couple_kernel,
        grid=(slot_count,),
        out_shape=pltpu.VMEM((slot_count, levels, blocks, rows, 2 * width), jnp.bfloat16),
        in_specs=[
            SMEM,
            pl.BlockSpec((1, levels, blocks, rows, width), lambda s: (s, 0, 0, 0, 0)),
        ],
        out_specs=VMEM,
        compiler_params=pltpu.CompilerParams(vmem_limit_bytes=8 * 1024 * 1024),
        cost_estimate=pl.CostEstimate(
            flops=COUPLE_FLOPS, bytes_accessed=2 * factors.size * 4, transcendentals=0
        ),
        name="couple",
    )(bound, in_hbm(factors))


def product(matrix, top, bottom):
    stacked = jnp.concatenate([top, bottom], axis=0)
    n = stacked.shape[1]
    wide = jnp.concatenate(halves(stacked), axis=1)
    wide = jnp.concatenate([wide, wide], axis=0)
    out = jnp.dot(matrix, wide, preferred_element_type=jnp.float32)
    return out[:, :n] + out[:, n:]


def butterfly_kernel(first, matrix_ref, own_ref, partner_ref, *refs):
    out_ref, done_ref = refs[-2:]
    done_ref[...] = jnp.zeros_like(done_ref)
    together = out_ref.shape[0]
    _, levels, blocks, rows, _ = matrix_ref.shape
    here = [pl.program_id(0) * together + t for t in range(together)]
    for i in range(blocks):
        for t in range(together):
            out_ref[t, i] = product(
                matrix_ref[here[t] + first, 0, i], own_ref[here[t], i], partner_ref[here[t], i]
            )
    for level in range(1, levels):
        dist = blocks >> level
        for i in range(blocks):
            for t in range(together):
                j = i ^ dist
                if i < j:
                    slot = here[t] + first
                    matrix = jnp.concatenate(
                        [matrix_ref[slot, level, i], matrix_ref[slot, level, j]], axis=0
                    )
                    both = product(matrix, out_ref[t, i], out_ref[t, j])
                    out_ref[t, i], out_ref[t, j] = both[:rows], both[rows:]


def butterfly(first, matrices, own, partner, so_far):
    count, blocks, rows, columns = own.shape
    slot_count, levels = matrices.shape[:2]
    together = max(t for t in range(1, TOGETHER + 1) if first % t == 0 and count % t == 0)
    args = [in_vmem(matrices), in_vmem(own), in_vmem(partner)]
    in_specs = [VMEM] * 3
    if so_far is not None:
        in_specs.append(ANY)
        args.append(so_far)
    return pl.pallas_call(
        functools.partial(butterfly_kernel, first),
        grid=(count // together,),
        out_shape=[
            jax.ShapeDtypeStruct((slot_count, blocks, rows, columns), own.dtype),
            pltpu.VMEM((8, columns), own.dtype),
        ],
        in_specs=in_specs,
        out_specs=[
            pl.BlockSpec(
                (together, blocks, rows, columns), lambda s: (s + first // together, 0, 0, 0)
            ),
            VMEM,
        ],
        input_output_aliases={} if so_far is None else {3: 0},
        compiler_params=pltpu.CompilerParams(vmem_limit_bytes=8 * 1024 * 1024),
        cost_estimate=pl.CostEstimate(
            flops=BUTTERFLY_FLOPS * count,
            bytes_accessed=0,
            transcendentals=0,
        ),
        name="butterfly",
    )(*args)


def coupling_bounds(slot_of_order, ranks, pattern, slot_count, blocks, rows):
    my_slots = lax.axis_index("order") * slot_count + jnp.arange(slot_count, dtype=jnp.int32)
    hits = (slot_of_order[None, :] == my_slots[:, None]).astype(jnp.int32)
    slot_rank = jnp.sum(hits[:, :, None] * ranks[None], axis=1)
    mine = lax.dynamic_slice_in_dim(pattern, lax.axis_index("lat") * blocks, blocks, 2)
    slot_pattern = jnp.sum(hits[:, :, None, None] * mine[None], axis=1)
    return (rows + slot_pattern * slot_rank[:, :, None]).reshape(-1)


def per_device(fourier, factors, slot_of_order, ranks, pattern):
    slot_count, _, blocks, block_rows, _ = factors.shape
    rows = fourier.shape[2]
    groups = lax.axis_size("order")
    bound = coupling_bounds(slot_of_order, ranks, pattern, slot_count, blocks, block_rows)
    swap = [(0, 1), (1, 0)]

    if rows % 8 or groups > 8 or groups & (groups - 1) or sum(CHUNKS[-1]) != slot_count:
        (packed,) = gather(((0, 0, slot_of_order.shape[0]),), 0, slot_of_order, fourier)
        own = lax.all_to_all(packed, "order", split_axis=0, concat_axis=2, tiled=True)
        return butterfly(0, couple(bound, factors), own, lax.ppermute(own, "lat", swap), None)[0]

    def hop(piece, k):
        return lax.ppermute(piece, "order", [(g, g ^ k) for g in range(groups)])

    half = groups // 2
    near = [(k, 0, slot_count) for k in range(1, half)]
    far = [(half + k, first, count) for k, first, count, _, _ in FAR]
    sent = gather([(0, 0, slot_count)] + near + far, slot_count, slot_of_order, fourier)
    got = {(0, 0, slot_count): sent[0]}
    for piece, step in zip(sent[1:], near):
        got[step] = hop(piece, step[0])
    matrices = couple(bound, factors)
    out, before, joined = None, matrices, []
    for c, (low, size) in enumerate(CHUNKS):
        for n, (piece, step, (_, _, _, when, wait)) in enumerate(zip(sent[half:], far, FAR)):
            if when == c:
                if wait is not None:
                    piece = after(piece, joined[~wait] if wait < 0 else got[far[wait]])
                    if n == EARLY:
                        piece = after(piece, matrices)
                got[step] = hop(piece, step[0])
        plan, pieces = [], []
        for (k, first, count), piece in got.items():
            if first <= low < first + count:
                plan.append((k, low - first))
                pieces.append(piece)
        own = join(plan, size, pieces, [before], out is None)
        joined.append(own)
        out, before = butterfly(low, matrices, own, lax.ppermute(own, "lat", swap), out)
    return out


def solution(mesh):
    return jax.shard_map(
        per_device,
        mesh=mesh,
        in_specs=(
            P("parts", "lat", "order", None),
            P("order", None, "lat", None, None),
            P(),
            P(),
            P(),
        ),
        out_specs=P(("parts", "order"), "lat", None, None),
        check_vma=False,
    )
```

```python
import functools

import jax
import jax.numpy as jnp
from jax import lax
from jax.experimental import pallas as pl
from jax.experimental.pallas import tpu as pltpu
from jax.sharding import PartitionSpec as P

LEVELS = 4
COUPLE_FLOPS = 30 * 10**9
LATE = 2
TOGETHER = 4
LAY_FLOPS = 100 * 10**9
ANY = pl.BlockSpec(memory_space=pl.ANY)
SMEM = pl.BlockSpec(memory_space=pltpu.SMEM)
VMEM = pl.BlockSpec(memory_space=pltpu.VMEM)


def in_vmem(x):
    return pltpu.with_memory_space_constraint(x, pltpu.VMEM)


def in_hbm(x):
    return pltpu.with_memory_space_constraint(x, pltpu.HBM)


def gather_kernel(plan, slot_count, slot_ref, rows_ref, *refs):
    outs, (slots, inverse, held, load_sem, held_sem) = refs[: len(plan)], refs[len(plan) :]
    me = lax.axis_index("order")
    load = pltpu.make_async_copy(slot_ref, slots, load_sem)
    load.start()
    fetch = pltpu.make_async_copy(rows_ref, held, held_sem)
    fetch.start()
    load.wait()

    def invert(m, carry):
        inverse[slots[m]] = m
        return carry

    lax.fori_loop(0, slots.shape[0], invert, 0, unroll=16)
    fetch.wait()
    for out, (hop, first, count) in zip(outs, plan):
        base = (me ^ hop) * slot_count + first

        def copy(t, carry, out=out, base=base):
            out[t] = held[inverse[base + t]]
            return carry

        lax.fori_loop(0, count, copy, 0, unroll=8)


def gather(plan, slot_count, slot_of_order, fourier):
    shapes = [pltpu.VMEM((count,) + fourier.shape[1:], fourier.dtype) for _, _, count in plan]
    size = sum(count for _, _, count in plan) * fourier[0].size * 4
    return pl.pallas_call(
        functools.partial(gather_kernel, plan, slot_count),
        out_shape=shapes,
        in_specs=[ANY, ANY],
        out_specs=[VMEM] * len(plan),
        scratch_shapes=[
            pltpu.SMEM(slot_of_order.shape, jnp.int32),
            pltpu.SMEM(slot_of_order.shape, jnp.int32),
            pltpu.VMEM(fourier.shape, fourier.dtype),
            pltpu.SemaphoreType.DMA,
            pltpu.SemaphoreType.DMA,
        ],
        compiler_params=pltpu.CompilerParams(vmem_limit_bytes=6 * 1024 * 1024),
        cost_estimate=pl.CostEstimate(flops=0, bytes_accessed=2 * size, transcendentals=0),
        name="gather_rows",
    )(in_hbm(slot_of_order), in_hbm(fourier))


def place(out, steps, pieces):
    me = lax.axis_index("order")
    for (hop, first, count), piece in zip(steps, pieces):
        rows = piece.shape[2]
        low = pl.multiple_of((me ^ hop) * rows, rows)
        out[first : first + count, :, pl.ds(low, rows), :] = piece[...]


def join_kernel(hops, *refs):
    pieces, out = refs[: len(hops)], refs[-1]
    me = lax.rem(lax.axis_index("order"), len(hops))
    for hop, piece in zip(hops, pieces):
        rows = piece.shape[2]
        low = pl.multiple_of((me ^ hop) * rows, rows)
        out[:, :, pl.ds(low, rows), :] = piece[...]


def join(hops, pieces):
    count, blocks, rows, columns = pieces[0].shape
    shape = (count, blocks, rows * len(hops), columns)
    return pl.pallas_call(
        functools.partial(join_kernel, hops),
        out_shape=pltpu.VMEM(shape, pieces[0].dtype),
        in_specs=[VMEM] * len(pieces),
        out_specs=VMEM,
        compiler_params=pltpu.CompilerParams(vmem_limit_bytes=4 * 1024 * 1024),
        cost_estimate=pl.CostEstimate(flops=0, bytes_accessed=0, transcendentals=0),
        name="join_near",
    )(*[in_vmem(piece) for piece in pieces])


def lay_kernel(steps, near, *refs):
    ins, outs = refs[: 2 * (len(steps) + 1)], refs[-2:]
    half = len(ins) // 2
    for out, group in zip(outs, (ins[:half], ins[half:])):
        rows = group[0].shape[2]
        low = pl.multiple_of(lax.div(lax.axis_index("order"), near) * rows, rows)
        out[:, :, pl.ds(low, rows), :] = group[0][...]
        place(out, steps, group[1:])


def lay(steps, near, rows, own, partner, before):
    count, blocks, _, columns = own[0].shape
    shape = pltpu.VMEM((count, blocks, rows, columns), own[0].dtype)
    return pl.pallas_call(
        functools.partial(lay_kernel, steps, near),
        out_shape=[shape, shape],
        in_specs=[VMEM] * (2 * len(own)) + [ANY] * len(before),
        out_specs=[VMEM] * 2,
        compiler_params=pltpu.CompilerParams(vmem_limit_bytes=4 * 1024 * 1024),
        cost_estimate=pl.CostEstimate(flops=LAY_FLOPS, bytes_accessed=0, transcendentals=0),
        name="lay_rows",
    )(*[in_vmem(x) for x in own + partner], *before)


def hand_on_kernel(*refs):
    del refs


def after(x, *arrived, flops=0):
    return pl.pallas_call(
        hand_on_kernel,
        out_shape=pltpu.VMEM(x.shape, x.dtype),
        in_specs=[ANY] * (1 + len(arrived)),
        out_specs=ANY,
        input_output_aliases={0: 0},
        compiler_params=pltpu.CompilerParams(vmem_limit_bytes=1024 * 1024),
        cost_estimate=pl.CostEstimate(flops=flops, bytes_accessed=0, transcendentals=0),
        name="hand_on",
    )(*[in_vmem(y) for y in (x,) + arrived])


def halves(x):
    high = x.astype(jnp.bfloat16)
    return high, (x - high.astype(jnp.float32)).astype(jnp.bfloat16)


def couple_kernel(bound_ref, factor_ref, out_ref):
    slot = pl.program_id(0)
    _, levels, blocks, rows, width = factor_ref.shape
    lanes = lax.broadcasted_iota(jnp.int32, (rows, width), 1)
    for level in range(levels):
        for i in range(blocks):
            keep = lanes < bound_ref[(slot * levels + level) * blocks + i]
            matrix = jnp.where(keep, factor_ref[0, level, i], 0.0)
            if level and i & (blocks >> level):
                matrix = pltpu.roll(matrix, rows, 1)
            high, low = halves(matrix)
            out_ref[slot, level, i, :, :width] = high
            out_ref[slot, level, i, :, width:] = low


def couple(bound, factors):
    slot_count, levels, blocks, rows, width = factors.shape
    return pl.pallas_call(
        couple_kernel,
        grid=(slot_count,),
        out_shape=pltpu.VMEM((slot_count, levels, blocks, rows, 2 * width), jnp.bfloat16),
        in_specs=[
            SMEM,
            pl.BlockSpec((1, levels, blocks, rows, width), lambda s: (s, 0, 0, 0, 0)),
        ],
        out_specs=VMEM,
        compiler_params=pltpu.CompilerParams(vmem_limit_bytes=8 * 1024 * 1024),
        cost_estimate=pl.CostEstimate(
            flops=COUPLE_FLOPS, bytes_accessed=2 * factors.size * 4, transcendentals=0
        ),
        name="couple",
    )(bound, in_hbm(factors))


def product(matrix, top, bottom):
    stacked = jnp.concatenate([top, bottom], axis=0)
    n = stacked.shape[1]
    wide = jnp.concatenate(halves(stacked), axis=1)
    wide = jnp.concatenate([wide, wide], axis=0)
    out = jnp.dot(matrix, wide, preferred_element_type=jnp.float32)
    return out[:, :n] + out[:, n:]


def butterfly_kernel(steps, matrix_ref, own_ref, partner_ref, *refs):
    pieces, out_ref = refs[: 2 * len(steps)], refs[2 * len(steps)]
    own, partner = refs[-2:]
    _, levels, blocks, rows, _ = matrix_ref.shape
    together = out_ref.shape[0]

    @pl.when(pl.program_id(0) == 0)
    def _():
        place(own, steps, pieces[: len(steps)])
        place(partner, steps, pieces[len(steps) :])

    slots = [pl.program_id(0) * together + t for t in range(together)]
    for i in range(blocks):
        for t, slot in enumerate(slots):
            out_ref[t, i] = product(matrix_ref[slot, 0, i], own[slot, i], partner[slot, i])
    for level in range(1, levels):
        dist = blocks >> level
        for i in range(blocks):
            for t, slot in enumerate(slots):
                j = i ^ dist
                if i < j:
                    matrix = jnp.concatenate(
                        [matrix_ref[slot, level, i], matrix_ref[slot, level, j]], axis=0
                    )
                    both = product(matrix, out_ref[t, i], out_ref[t, j])
                    out_ref[t, i], out_ref[t, j] = both[:rows], both[rows:]


def butterfly(steps, matrices, own, partner, own_pieces, partner_pieces):
    count, blocks, rows, columns = own.shape
    args = [matrices, own, partner] + own_pieces + partner_pieces
    state = pltpu.VMEM(own.shape, own.dtype)
    together = max(t for t in range(1, TOGETHER + 1) if count % t == 0)
    return pl.pallas_call(
        functools.partial(butterfly_kernel, steps),
        grid=(count // together,),
        out_shape=[jax.ShapeDtypeStruct(own.shape, own.dtype), state, state],
        in_specs=[VMEM] * len(args),
        out_specs=[
            pl.BlockSpec((together, blocks, rows, columns), lambda s: (s, 0, 0, 0)),
            VMEM,
            VMEM,
        ],
        input_output_aliases={1: 1, 2: 2},
        compiler_params=pltpu.CompilerParams(vmem_limit_bytes=12 * 1024 * 1024),
        cost_estimate=pl.CostEstimate(flops=0, bytes_accessed=0, transcendentals=0),
        name="butterfly",
    )(*[in_vmem(x) for x in args])[0]


def coupling_bounds(slot_of_order, ranks, pattern, slot_count, blocks, rows):
    my_slots = lax.axis_index("order") * slot_count + jnp.arange(slot_count, dtype=jnp.int32)
    hits = (slot_of_order[None, :] == my_slots[:, None]).astype(jnp.int32)
    slot_rank = jnp.sum(hits[:, :, None] * ranks[None], axis=1)
    mine = lax.dynamic_slice_in_dim(pattern, lax.axis_index("lat") * blocks, blocks, 2)
    slot_pattern = jnp.sum(hits[:, :, None, None] * mine[None], axis=1)
    return (rows + slot_pattern * slot_rank[:, :, None]).reshape(-1)


def per_device(fourier, factors, slot_of_order, ranks, pattern):
    slot_count, _, blocks, block_rows, _ = factors.shape
    rows = fourier.shape[2]
    groups = lax.axis_size("order")
    bound = coupling_bounds(slot_of_order, ranks, pattern, slot_count, blocks, block_rows)
    swap = [(0, 1), (1, 0)]

    matrices = couple(bound, factors)

    def over(piece):
        return lax.ppermute(piece, "lat", swap)

    if rows % 8 or groups != 8 or slot_count < 2:
        (packed,) = gather(((0, 0, slot_of_order.shape[0]),), 0, slot_of_order, fourier)
        own = lax.all_to_all(packed, "order", split_axis=0, concat_axis=2, tiled=True)
        return butterfly([], matrices, own, over(own), [], [])

    def hop(piece, k):
        return lax.ppermute(piece, "order", [(g, g ^ k) for g in range(groups)])

    half, head = groups // 2, max(1, 3 * slot_count // 8)
    near = [(k, 0, slot_count) for k in range(half)]
    far = [
        ((half, 0, head), None),
        ((half + 1, 0, slot_count), None),
        ((half + 2, 0, slot_count), 0),
        ((half, head, slot_count - head), 1),
        ((half + 3, 0, slot_count), 2),
    ]
    waits, far = [wait for _, wait in far], [step for step, _ in far]
    sent = list(gather(near + far, slot_count, slot_of_order, fourier))
    got = []
    for piece, (k, _, _), wait in zip(sent[half:], far, waits):
        got.append(hop(piece if wait is None else after(piece, got[wait]), k))
    close = [hop(sent[k], k) for k in range(1, half)]
    close = join(range(half), sent[:1] + close)
    swapped = [over(piece) for piece in got]
    own, partner = lay(
        far[:-LATE], half, block_rows, [close] + got[:-LATE], [over(close)] + swapped[:-LATE], [matrices]
    )
    return butterfly(far[-LATE:], matrices, own, partner, got[-LATE:], swapped[-LATE:])


def solution(mesh):
    return jax.shard_map(
        per_device,
        mesh=mesh,
        in_specs=(
            P("parts", "lat", "order", None),
            P("order", None, "lat", None, None),
            P(),
            P(),
            P(),
        ),
        out_specs=P(("parts", "order"), "lat", None, None),
        check_vma=False,
    )
```

```python
import functools

import jax
import jax.numpy as jnp
from jax import lax
from jax.experimental import pallas as pl
from jax.experimental.pallas import tpu as pltpu
from jax.sharding import PartitionSpec as P

LEVELS = 4
COUPLE_FLOPS = 30 * 10**9
LATE = 2
TOGETHER = 4
LAY_FLOPS = 100 * 10**9
ANY = pl.BlockSpec(memory_space=pl.ANY)
SMEM = pl.BlockSpec(memory_space=pltpu.SMEM)
VMEM = pl.BlockSpec(memory_space=pltpu.VMEM)


def in_vmem(x):
    return pltpu.with_memory_space_constraint(x, pltpu.VMEM)


def in_hbm(x):
    return pltpu.with_memory_space_constraint(x, pltpu.HBM)


def gather_kernel(plan, slot_count, slot_ref, rows_ref, *refs):
    outs, (slots, inverse, held, load_sem, held_sem) = refs[: len(plan)], refs[len(plan) :]
    me = lax.axis_index("order")
    load = pltpu.make_async_copy(slot_ref, slots, load_sem)
    load.start()
    fetch = pltpu.make_async_copy(rows_ref, held, held_sem)
    fetch.start()
    load.wait()

    def invert(m, carry):
        inverse[slots[m]] = m
        return carry

    lax.fori_loop(0, slots.shape[0], invert, 0, unroll=16)
    fetch.wait()
    for out, (hop, first, count) in zip(outs, plan):
        base = (me ^ hop) * slot_count + first

        def copy(t, carry, out=out, base=base):
            out[t] = held[inverse[base + t]]
            return carry

        lax.fori_loop(0, count, copy, 0, unroll=8)


def gather(plan, slot_count, slot_of_order, fourier):
    shapes = [pltpu.VMEM((count,) + fourier.shape[1:], fourier.dtype) for _, _, count in plan]
    size = sum(count for _, _, count in plan) * fourier[0].size * 4
    return pl.pallas_call(
        functools.partial(gather_kernel, plan, slot_count),
        out_shape=shapes,
        in_specs=[ANY, ANY],
        out_specs=[VMEM] * len(plan),
        scratch_shapes=[
            pltpu.SMEM(slot_of_order.shape, jnp.int32),
            pltpu.SMEM(slot_of_order.shape, jnp.int32),
            pltpu.VMEM(fourier.shape, fourier.dtype),
            pltpu.SemaphoreType.DMA,
            pltpu.SemaphoreType.DMA,
        ],
        compiler_params=pltpu.CompilerParams(vmem_limit_bytes=6 * 1024 * 1024),
        cost_estimate=pl.CostEstimate(flops=0, bytes_accessed=2 * size, transcendentals=0),
        name="gather_rows",
    )(in_hbm(slot_of_order), in_hbm(fourier))


def place(out, steps, pieces):
    me = lax.axis_index("order")
    for (hop, first, count), piece in zip(steps, pieces):
        rows = piece.shape[2]
        low = pl.multiple_of((me ^ hop) * rows, rows)
        out[first : first + count, :, pl.ds(low, rows), :] = piece[...]


def join_kernel(hops, *refs):
    pieces, out = refs[: len(hops)], refs[-1]
    me = lax.rem(lax.axis_index("order"), len(hops))
    for hop, piece in zip(hops, pieces):
        rows = piece.shape[2]
        low = pl.multiple_of((me ^ hop) * rows, rows)
        out[:, :, pl.ds(low, rows), :] = piece[...]


def join(hops, pieces):
    count, blocks, rows, columns = pieces[0].shape
    shape = (count, blocks, rows * len(hops), columns)
    return pl.pallas_call(
        functools.partial(join_kernel, hops),
        out_shape=pltpu.VMEM(shape, pieces[0].dtype),
        in_specs=[VMEM] * len(pieces),
        out_specs=VMEM,
        compiler_params=pltpu.CompilerParams(vmem_limit_bytes=4 * 1024 * 1024),
        cost_estimate=pl.CostEstimate(flops=0, bytes_accessed=0, transcendentals=0),
        name="join_near",
    )(*[in_vmem(piece) for piece in pieces])


def lay_kernel(steps, near, *refs):
    ins, outs = refs[: 2 * (len(steps) + 1)], refs[-2:]
    half = len(ins) // 2
    for out, group in zip(outs, (ins[:half], ins[half:])):
        rows = group[0].shape[2]
        low = pl.multiple_of(lax.div(lax.axis_index("order"), near) * rows, rows)
        out[:, :, pl.ds(low, rows), :] = group[0][...]
        place(out, steps, group[1:])


def lay(steps, near, rows, own, partner, before):
    count, blocks, _, columns = own[0].shape
    shape = pltpu.VMEM((count, blocks, rows, columns), own[0].dtype)
    return pl.pallas_call(
        functools.partial(lay_kernel, steps, near),
        out_shape=[shape, shape],
        in_specs=[VMEM] * (2 * len(own)) + [ANY] * len(before),
        out_specs=[VMEM] * 2,
        compiler_params=pltpu.CompilerParams(vmem_limit_bytes=4 * 1024 * 1024),
        cost_estimate=pl.CostEstimate(flops=LAY_FLOPS, bytes_accessed=0, transcendentals=0),
        name="lay_rows",
    )(*[in_vmem(x) for x in own + partner], *before)


def hand_on_kernel(*refs):
    del refs


def after(x, *arrived, flops=0):
    return pl.pallas_call(
        hand_on_kernel,
        out_shape=pltpu.VMEM(x.shape, x.dtype),
        in_specs=[ANY] * (1 + len(arrived)),
        out_specs=ANY,
        input_output_aliases={0: 0},
        compiler_params=pltpu.CompilerParams(vmem_limit_bytes=1024 * 1024),
        cost_estimate=pl.CostEstimate(flops=flops, bytes_accessed=0, transcendentals=0),
        name="hand_on",
    )(*[in_vmem(y) for y in (x,) + arrived])


def halves(x):
    high = x.astype(jnp.bfloat16)
    return high, (x - high.astype(jnp.float32)).astype(jnp.bfloat16)


def couple_kernel(bound_ref, factor_ref, out_ref):
    slot = pl.program_id(0)
    _, levels, blocks, rows, width = factor_ref.shape
    lanes = lax.broadcasted_iota(jnp.int32, (rows, width), 1)
    for level in range(levels):
        for i in range(blocks):
            keep = lanes < bound_ref[(slot * levels + level) * blocks + i]
            matrix = jnp.where(keep, factor_ref[0, level, i], 0.0)
            if level and i & (blocks >> level):
                matrix = pltpu.roll(matrix, rows, 1)
            high, low = halves(matrix)
            out_ref[slot, level, i, :, :width] = high
            out_ref[slot, level, i, :, width:] = low


def couple(bound, factors):
    slot_count, levels, blocks, rows, width = factors.shape
    return pl.pallas_call(
        couple_kernel,
        grid=(slot_count,),
        out_shape=pltpu.VMEM((slot_count, levels, blocks, rows, 2 * width), jnp.bfloat16),
        in_specs=[
            SMEM,
            pl.BlockSpec((1, levels, blocks, rows, width), lambda s: (s, 0, 0, 0, 0)),
        ],
        out_specs=VMEM,
        compiler_params=pltpu.CompilerParams(vmem_limit_bytes=8 * 1024 * 1024),
        cost_estimate=pl.CostEstimate(
            flops=COUPLE_FLOPS, bytes_accessed=2 * factors.size * 4, transcendentals=0
        ),
        name="couple",
    )(bound, in_hbm(factors))


def product(matrix, top, bottom):
    stacked = jnp.concatenate([top, bottom], axis=0)
    n = stacked.shape[1]
    wide = jnp.concatenate(halves(stacked), axis=1)
    wide = jnp.concatenate([wide, wide], axis=0)
    out = jnp.dot(matrix, wide, preferred_element_type=jnp.float32)
    return out[:, :n] + out[:, n:]


def butterfly_kernel(steps, matrix_ref, own_ref, partner_ref, *refs):
    pieces, (out_ref, own, partner, state, sems) = refs[: 2 * len(steps)], refs[-5:]
    slot_count, levels, blocks, rows, _ = matrix_ref.shape
    place(own, steps, pieces[: len(steps)])
    place(partner, steps, pieces[len(steps) :])

    def pair(level, i, slot):
        j = i ^ (blocks >> level)
        if i < j:
            matrix = jnp.concatenate([matrix_ref[slot, level, i], matrix_ref[slot, level, j]], axis=0)
            both = product(matrix, state[slot, i], state[slot, j])
            state[slot, i], state[slot, j] = both[:rows], both[rows:]

    copies = []
    for low in range(0, slot_count, TOGETHER):
        slots = range(low, min(low + TOGETHER, slot_count))
        for i in range(blocks):
            for slot in slots:
                state[slot, i] = product(matrix_ref[slot, 0, i], own[slot, i], partner[slot, i])
        for level in range(1, levels - 1):
            for i in range(blocks):
                for slot in slots:
                    pair(level, i, slot)
        for slot in slots:
            for i in range(blocks):
                pair(levels - 1, i, slot)
            copies.append(pltpu.make_async_copy(state.at[slot], out_ref.at[slot], sems.at[slot]))
            copies[-1].start()
    for copy in copies:
        copy.wait()


def butterfly(steps, matrices, own, partner, own_pieces, partner_pieces):
    args = [matrices, own, partner] + own_pieces + partner_pieces
    state = pltpu.VMEM(own.shape, own.dtype)
    return pl.pallas_call(
        functools.partial(butterfly_kernel, steps),
        out_shape=[pltpu.HBM(own.shape, own.dtype), state, state],
        in_specs=[VMEM] * len(args),
        out_specs=[ANY, VMEM, VMEM],
        scratch_shapes=[state, pltpu.SemaphoreType.DMA((own.shape[0],))],
        input_output_aliases={1: 1, 2: 2},
        compiler_params=pltpu.CompilerParams(vmem_limit_bytes=12 * 1024 * 1024),
        cost_estimate=pl.CostEstimate(flops=0, bytes_accessed=0, transcendentals=0),
        name="butterfly",
    )(*[in_vmem(x) for x in args])[0]


def coupling_bounds(slot_of_order, ranks, pattern, slot_count, blocks, rows):
    my_slots = lax.axis_index("order") * slot_count + jnp.arange(slot_count, dtype=jnp.int32)
    hits = (slot_of_order[None, :] == my_slots[:, None]).astype(jnp.int32)
    slot_rank = jnp.sum(hits[:, :, None] * ranks[None], axis=1)
    mine = lax.dynamic_slice_in_dim(pattern, lax.axis_index("lat") * blocks, blocks, 2)
    slot_pattern = jnp.sum(hits[:, :, None, None] * mine[None], axis=1)
    return (rows + slot_pattern * slot_rank[:, :, None]).reshape(-1)


def per_device(fourier, factors, slot_of_order, ranks, pattern):
    slot_count, _, blocks, block_rows, _ = factors.shape
    rows = fourier.shape[2]
    groups = lax.axis_size("order")
    bound = coupling_bounds(slot_of_order, ranks, pattern, slot_count, blocks, block_rows)
    swap = [(0, 1), (1, 0)]

    matrices = couple(bound, factors)

    def over(piece):
        return lax.ppermute(piece, "lat", swap)

    if rows % 8 or groups != 8 or slot_count < 2:
        (packed,) = gather(((0, 0, slot_of_order.shape[0]),), 0, slot_of_order, fourier)
        own = lax.all_to_all(packed, "order", split_axis=0, concat_axis=2, tiled=True)
        return butterfly([], matrices, own, over(own), [], [])

    def hop(piece, k):
        return lax.ppermute(piece, "order", [(g, g ^ k) for g in range(groups)])

    half, head = groups // 2, max(1, 3 * slot_count // 8)
    near = [(k, 0, slot_count) for k in range(half)]
    far = [
        ((half, 0, head), None),
        ((half + 1, 0, slot_count), None),
        ((half + 2, 0, slot_count), 0),
        ((half, head, slot_count - head), 1),
        ((half + 3, 0, slot_count), 2),
    ]
    waits, far = [wait for _, wait in far], [step for step, _ in far]
    sent = list(gather(near + far, slot_count, slot_of_order, fourier))
    got = []
    for piece, (k, _, _), wait in zip(sent[half:], far, waits):
        got.append(hop(piece if wait is None else after(piece, got[wait]), k))
    close = [hop(sent[k], k) for k in range(1, half)]
    close = join(range(half), sent[:1] + close)
    swapped = [over(piece) for piece in got]
    own, partner = lay(
        far[:-LATE], half, block_rows, [close] + got[:-LATE], [over(close)] + swapped[:-LATE], [matrices]
    )
    return butterfly(far[-LATE:], matrices, own, partner, got[-LATE:], swapped[-LATE:])


def solution(mesh):
    return jax.shard_map(
        per_device,
        mesh=mesh,
        in_specs=(
            P("parts", "lat", "order", None),
            P("order", None, "lat", None, None),
            P(),
            P(),
            P(),
        ),
        out_specs=P(("parts", "order"), "lat", None, None),
        check_vma=False,
    )
```

```python
import functools

import jax
import jax.numpy as jnp
from jax import lax
from jax.experimental import pallas as pl
from jax.experimental.pallas import tpu as pltpu
from jax.sharding import PartitionSpec as P

LEVELS = 4
COUPLE_FLOPS = 30 * 10**9
LATE = 2
TOGETHER = 4
LAY_FLOPS = 100 * 10**9
ANY = pl.BlockSpec(memory_space=pl.ANY)
SMEM = pl.BlockSpec(memory_space=pltpu.SMEM)
VMEM = pl.BlockSpec(memory_space=pltpu.VMEM)


def in_vmem(x):
    return pltpu.with_memory_space_constraint(x, pltpu.VMEM)


def in_hbm(x):
    return pltpu.with_memory_space_constraint(x, pltpu.HBM)


def gather_kernel(plan, slot_count, slot_ref, rows_ref, *refs):
    outs, (slots, inverse, held, load_sem, held_sem) = refs[: len(plan)], refs[len(plan) :]
    me = lax.axis_index("order")
    load = pltpu.make_async_copy(slot_ref, slots, load_sem)
    load.start()
    fetch = pltpu.make_async_copy(rows_ref, held, held_sem)
    fetch.start()
    load.wait()

    def invert(m, carry):
        inverse[slots[m]] = m
        return carry

    lax.fori_loop(0, slots.shape[0], invert, 0, unroll=16)
    fetch.wait()
    for out, (hop, first, count) in zip(outs, plan):
        base = (me ^ hop) * slot_count + first

        def copy(t, carry, out=out, base=base):
            out[t] = held[inverse[base + t]]
            return carry

        lax.fori_loop(0, count, copy, 0, unroll=8)


def gather(plan, slot_count, slot_of_order, fourier):
    shapes = [pltpu.VMEM((count,) + fourier.shape[1:], fourier.dtype) for _, _, count in plan]
    size = sum(count for _, _, count in plan) * fourier[0].size * 4
    return pl.pallas_call(
        functools.partial(gather_kernel, plan, slot_count),
        out_shape=shapes,
        in_specs=[ANY, ANY],
        out_specs=[VMEM] * len(plan),
        scratch_shapes=[
            pltpu.SMEM(slot_of_order.shape, jnp.int32),
            pltpu.SMEM(slot_of_order.shape, jnp.int32),
            pltpu.VMEM(fourier.shape, fourier.dtype),
            pltpu.SemaphoreType.DMA,
            pltpu.SemaphoreType.DMA,
        ],
        compiler_params=pltpu.CompilerParams(vmem_limit_bytes=6 * 1024 * 1024),
        cost_estimate=pl.CostEstimate(flops=0, bytes_accessed=2 * size, transcendentals=0),
        name="gather_rows",
    )(in_hbm(slot_of_order), in_hbm(fourier))


def place(out, steps, pieces):
    me = lax.axis_index("order")
    for (hop, first, count), piece in zip(steps, pieces):
        rows = piece.shape[2]
        low = pl.multiple_of((me ^ hop) * rows, rows)
        out[first : first + count, :, pl.ds(low, rows), :] = piece[...]


def join_kernel(hops, *refs):
    pieces, out = refs[: len(hops)], refs[-1]
    me = lax.rem(lax.axis_index("order"), len(hops))
    for hop, piece in zip(hops, pieces):
        rows = piece.shape[2]
        low = pl.multiple_of((me ^ hop) * rows, rows)
        out[:, :, pl.ds(low, rows), :] = piece[...]


def join(hops, pieces):
    count, blocks, rows, columns = pieces[0].shape
    shape = (count, blocks, rows * len(hops), columns)
    return pl.pallas_call(
        functools.partial(join_kernel, hops),
        out_shape=pltpu.VMEM(shape, pieces[0].dtype),
        in_specs=[VMEM] * len(pieces),
        out_specs=VMEM,
        compiler_params=pltpu.CompilerParams(vmem_limit_bytes=4 * 1024 * 1024),
        cost_estimate=pl.CostEstimate(flops=0, bytes_accessed=0, transcendentals=0),
        name="join_near",
    )(*[in_vmem(piece) for piece in pieces])


def lay_kernel(steps, near, *refs):
    ins, outs = refs[: 2 * (len(steps) + 1)], refs[-2:]
    half = len(ins) // 2
    for out, group in zip(outs, (ins[:half], ins[half:])):
        rows = group[0].shape[2]
        low = pl.multiple_of(lax.div(lax.axis_index("order"), near) * rows, rows)
        out[:, :, pl.ds(low, rows), :] = group[0][...]
        place(out, steps, group[1:])


def lay(steps, near, rows, own, partner, before):
    count, blocks, _, columns = own[0].shape
    shape = pltpu.VMEM((count, blocks, rows, columns), own[0].dtype)
    return pl.pallas_call(
        functools.partial(lay_kernel, steps, near),
        out_shape=[shape, shape],
        in_specs=[VMEM] * (2 * len(own)) + [ANY] * len(before),
        out_specs=[VMEM] * 2,
        compiler_params=pltpu.CompilerParams(vmem_limit_bytes=4 * 1024 * 1024),
        cost_estimate=pl.CostEstimate(flops=LAY_FLOPS, bytes_accessed=0, transcendentals=0),
        name="lay_rows",
    )(*[in_vmem(x) for x in own + partner], *before)


def hand_on_kernel(*refs):
    del refs


def after(x, *arrived, flops=0):
    return pl.pallas_call(
        hand_on_kernel,
        out_shape=pltpu.VMEM(x.shape, x.dtype),
        in_specs=[ANY] * (1 + len(arrived)),
        out_specs=ANY,
        input_output_aliases={0: 0},
        compiler_params=pltpu.CompilerParams(vmem_limit_bytes=1024 * 1024),
        cost_estimate=pl.CostEstimate(flops=flops, bytes_accessed=0, transcendentals=0),
        name="hand_on",
    )(*[in_vmem(y) for y in (x,) + arrived])


def halves(x):
    high = x.astype(jnp.bfloat16)
    return high, (x - high.astype(jnp.float32)).astype(jnp.bfloat16)


def couple_kernel(bound_ref, factor_ref, out_ref):
    slot = pl.program_id(0)
    _, levels, blocks, rows, width = factor_ref.shape
    lanes = lax.broadcasted_iota(jnp.int32, (rows, width), 1)
    for level in range(levels):
        for i in range(blocks):
            keep = lanes < bound_ref[(slot * levels + level) * blocks + i]
            matrix = jnp.where(keep, factor_ref[0, level, i], 0.0)
            if level and i & (blocks >> level):
                matrix = pltpu.roll(matrix, rows, 1)
            high, low = halves(matrix)
            out_ref[slot, level, i, :, :width] = high
            out_ref[slot, level, i, :, width:] = low


def couple(bound, factors):
    slot_count, levels, blocks, rows, width = factors.shape
    return pl.pallas_call(
        couple_kernel,
        grid=(slot_count,),
        out_shape=pltpu.VMEM((slot_count, levels, blocks, rows, 2 * width), jnp.bfloat16),
        in_specs=[
            SMEM,
            pl.BlockSpec((1, levels, blocks, rows, width), lambda s: (s, 0, 0, 0, 0)),
        ],
        out_specs=VMEM,
        compiler_params=pltpu.CompilerParams(vmem_limit_bytes=8 * 1024 * 1024),
        cost_estimate=pl.CostEstimate(
            flops=COUPLE_FLOPS, bytes_accessed=2 * factors.size * 4, transcendentals=0
        ),
        name="couple",
    )(bound, in_hbm(factors))


def product(matrix, top, bottom):
    stacked = jnp.concatenate([top, bottom], axis=0)
    n = stacked.shape[1]
    wide = jnp.concatenate(halves(stacked), axis=1)
    wide = jnp.concatenate([wide, wide], axis=0)
    out = jnp.dot(matrix, wide, preferred_element_type=jnp.float32)
    return out[:, :n] + out[:, n:]


def butterfly_kernel(steps, matrix_ref, own_ref, partner_ref, *refs):
    pieces, (out_ref, own, partner, state, sems) = refs[: 2 * len(steps)], refs[-5:]
    slot_count, levels, blocks, rows, _ = matrix_ref.shape
    place(own, steps, pieces[: len(steps)])
    place(partner, steps, pieces[len(steps) :])

    def pair(level, i, slot):
        j = i ^ (blocks >> level)
        if i < j:
            matrix = jnp.concatenate([matrix_ref[slot, level, i], matrix_ref[slot, level, j]], axis=0)
            both = product(matrix, state[slot, i], state[slot, j])
            state[slot, i], state[slot, j] = both[:rows], both[rows:]

    copies = []
    for low in range(0, slot_count, TOGETHER):
        slots = range(low, min(low + TOGETHER, slot_count))
        for i in range(blocks):
            for slot in slots:
                state[slot, i] = product(matrix_ref[slot, 0, i], own[slot, i], partner[slot, i])
        for level in range(1, levels - 1):
            for i in range(blocks):
                for slot in slots:
                    pair(level, i, slot)
        for slot in slots:
            for i in range(blocks):
                pair(levels - 1, i, slot)
            copies.append(pltpu.make_async_copy(state.at[slot], out_ref.at[slot], sems.at[slot]))
            copies[-1].start()
    for copy in copies:
        copy.wait()


def butterfly(steps, matrices, own, partner, own_pieces, partner_pieces):
    args = [matrices, own, partner] + own_pieces + partner_pieces
    state = pltpu.VMEM(own.shape, own.dtype)
    return pl.pallas_call(
        functools.partial(butterfly_kernel, steps),
        out_shape=[pltpu.HBM(own.shape, own.dtype), state, state],
        in_specs=[VMEM] * len(args),
        out_specs=[ANY, VMEM, VMEM],
        scratch_shapes=[state, pltpu.SemaphoreType.DMA((own.shape[0],))],
        input_output_aliases={1: 1, 2: 2},
        compiler_params=pltpu.CompilerParams(vmem_limit_bytes=12 * 1024 * 1024),
        cost_estimate=pl.CostEstimate(flops=0, bytes_accessed=0, transcendentals=0),
        name="butterfly",
    )(*[in_vmem(x) for x in args])[0]


def coupling_bounds(slot_of_order, ranks, pattern, slot_count, blocks, rows):
    my_slots = lax.axis_index("order") * slot_count + jnp.arange(slot_count, dtype=jnp.int32)
    hits = (slot_of_order[None, :] == my_slots[:, None]).astype(jnp.int32)
    slot_rank = jnp.sum(hits[:, :, None] * ranks[None], axis=1)
    mine = lax.dynamic_slice_in_dim(pattern, lax.axis_index("lat") * blocks, blocks, 2)
    slot_pattern = jnp.sum(hits[:, :, None, None] * mine[None], axis=1)
    return (rows + slot_pattern * slot_rank[:, :, None]).reshape(-1)


def per_device(fourier, factors, slot_of_order, ranks, pattern):
    slot_count, _, blocks, block_rows, _ = factors.shape
    rows = fourier.shape[2]
    groups = lax.axis_size("order")
    bound = coupling_bounds(slot_of_order, ranks, pattern, slot_count, blocks, block_rows)
    swap = [(0, 1), (1, 0)]

    matrices = couple(bound, factors)

    def over(piece):
        return lax.ppermute(piece, "lat", swap)

    if rows % 8 or groups != 8 or slot_count < 2:
        (packed,) = gather(((0, 0, slot_of_order.shape[0]),), 0, slot_of_order, fourier)
        own = lax.all_to_all(packed, "order", split_axis=0, concat_axis=2, tiled=True)
        return butterfly([], matrices, own, over(own), [], [])

    def hop(piece, k):
        return lax.ppermute(piece, "order", [(g, g ^ k) for g in range(groups)])

    half, head = groups // 2, max(1, slot_count // 2)
    near = [(k, 0, slot_count) for k in range(half)]
    far = [
        ((half, 0, head), None),
        ((half + 1, 0, slot_count), None),
        ((half + 2, 0, slot_count), 0),
        ((half, head, slot_count - head), 1),
        ((half + 3, 0, slot_count), 2),
    ]
    waits, far = [wait for _, wait in far], [step for step, _ in far]
    sent = list(gather(near + far, slot_count, slot_of_order, fourier))
    got = []
    for piece, (k, _, _), wait in zip(sent[half:], far, waits):
        got.append(hop(piece if wait is None else after(piece, got[wait]), k))
    close = [hop(sent[k], k) for k in range(1, half)]
    close = join(range(half), sent[:1] + close)
    swapped = [over(piece) for piece in got]
    own, partner = lay(
        far[:-LATE], half, block_rows, [close] + got[:-LATE], [over(close)] + swapped[:-LATE], [matrices]
    )
    return butterfly(far[-LATE:], matrices, own, partner, got[-LATE:], swapped[-LATE:])


def solution(mesh):
    return jax.shard_map(
        per_device,
        mesh=mesh,
        in_specs=(
            P("parts", "lat", "order", None),
            P("order", None, "lat", None, None),
            P(),
            P(),
            P(),
        ),
        out_specs=P(("parts", "order"), "lat", None, None),
        check_vma=False,
    )
```
